32 devices in a mesh: dp: 8 (over y, x, core), mp: 4 (over z).
Axes of the slice: x: 2, y: 2, z: 4, core: 2. Of those that a mesh axis runs over, the one named last changes fastest.
Arguments:
- hidden: bfloat16 [4096, 4096], P('dp', 'mp'), may hold values from -50 to 50
- norm_gain: float32 [4096], replicated, may hold values from 0.1 to 1.9
- w_query: bfloat16 [4096, 4096], P(None, 'mp'), may hold values from -0.09375 to 0.09375
- w_out: bfloat16 [4096, 4096], P('mp'), may hold values from -0.09375 to 0.09375
- nb_keys: bfloat16 [64, 128, 4096], P('dp', None, 'mp'), may hold values from -250 to 250
- nb_values: bfloat16 [64, 128, 4096], P('dp', None, 'mp'), may hold values from -10 to 10
- neighbours: int32 [64, 2], P('dp'), may hold values from 0 to 63, as said below
- valid_spans: int32 [8], P('dp'), may hold values from 6 to 8, as said below
Outputs:
- mixed: float32 [4096, 4096], P('dp', 'mp')
The draws below stay inside these ranges and needn't reach their ends.
Inputs may be any that keep to these rules, and one draw needn't show every extreme that they name: Block ids; block b is stored by index b // 8 of dp, its owner. The two neighbours of a span have different owners. The spans of one index of dp name one owner at most 2 times, and some owner is named exactly 2 times by the live spans of every index of dp. `valid_spans`: some index of dp has all 8 spans live.
All inputs are finite; a program needn't handle non-finite values.
Results may differ from the reference program's by a relative error of at most 0.0066.
Values may be sent and summed in bfloat16 or wider, within the bound.
A program may use at most 128 MiB of HBM per device.

```python
import math
import jax
import jax.numpy as jnp
from jax import lax

D = 4096
HEADS = 32
HS = 128
SPAN = 64
NBR = 128
NB_DEV = 8
HQ = 4096
SPAN_DEV = 8
MOST = 2
TOKENS = 4096
SPANS = 64
NBLOCKS = 64


def draw_hidden(key, part):
    key_base, key_rows, key_cols = jax.random.split(key, 3)
    row_scale = jnp.exp(jax.random.uniform(key_rows, (TOKENS, 1), jnp.float32, 0.0, math.log(10.0)))
    col_scale = jnp.exp(jax.random.uniform(key_cols, (1, D), jnp.float32, 0.0, math.log(10.0)))
    base_draw = jax.random.normal(key_base, (TOKENS, D), jnp.float32)
    return (jnp.clip(base_draw, -5.0, 5.0) * row_scale * col_scale * 0.1).astype(jnp.bfloat16)


def draw_nb_keys(key, part):
    key_base = jax.random.fold_in(key, 0)
    array_shape = (NBLOCKS, NBR, HEADS * HS)
    base_draw = jnp.clip(jax.random.normal(key_base, array_shape, jnp.float32), -5.0, 5.0)
    return base_draw.astype(jnp.bfloat16)


def one_order(sub_key):
    return jax.random.permutation(sub_key, NBLOCKS // NB_DEV - 1)


def draw_neighbours(key, part):
    key_special, key_perm, key_groups, key_slots = jax.random.split(key, 4)
    owner_count = NBLOCKS // NB_DEV
    per_device = SPAN_DEV
    special = jax.random.randint(key_special, (), 0, owner_count)
    shuffled = jax.vmap(one_order)(jax.random.split(key_perm, owner_count)).astype(jnp.int32)
    owner_queue = jnp.concatenate([jnp.full((owner_count, 1), special, jnp.int32), (special + 1 + shuffled) % owner_count], axis=1)
    lowest = max(1, -((owner_count - 2 * per_device) // (MOST - 1)))
    highest = min(owner_count, 2 * per_device // MOST)
    group_count = jax.random.randint(key_groups, (owner_count, 1), lowest, highest + 1)
    position = jnp.arange(2 * per_device, dtype=jnp.int32)[None, :]
    picked = jnp.where(position < MOST * group_count, position // MOST, group_count + position - MOST * group_count)
    owners = jnp.take_along_axis(owner_queue, picked, axis=1)
    chosen = jnp.stack([owners[:, :per_device], owners[:, per_device:]], axis=-1)
    slot_ids = jax.random.randint(key_slots, (owner_count, per_device, 2), 0, NB_DEV)
    return (chosen * NB_DEV + slot_ids).reshape(SPANS, 2).astype(jnp.int32)


def draw_valid_spans(key, part):
    key_counts, key_full, key_low = jax.random.split(key, 3)
    owner_count = NBLOCKS // NB_DEV
    lowest = 3 * SPAN_DEV // 4
    counts = jax.random.randint(key_counts, (owner_count,), lowest, SPAN_DEV + 1)
    full_device = jax.random.randint(key_full, (), 0, owner_count)
    low_device = (full_device + 1 + jax.random.randint(key_low, (), 0, owner_count - 1)) % owner_count
    device_index = jnp.arange(owner_count, dtype=jnp.int32)
    counts = jnp.where(device_index == full_device, SPAN_DEV, jnp.where(device_index == low_device, lowest, counts))
    return counts.astype(jnp.int32)


def shard_levels(rng, dims, cuts, smallest, top_value):
    def one(dim, parts):
        heights = jax.random.uniform(jax.random.fold_in(jax.random.fold_in(rng, 6), dim), (parts,), jnp.float32, smallest / len(cuts), top_value / len(cuts))
        return jnp.repeat(jnp.exp(heights), dims[dim] // parts).reshape((-1,) + (1,) * (len(dims) - dim - 1))

    gain = one(*cuts[0])
    for cut in cuts[1:]:
        gain = gain * one(*cut)
    return gain


def scatter_about(own_key, dims, scale, most, shards=(), kind=jnp.bfloat16):
    values = jax.random.normal(own_key, dims, jnp.float32) * scale
    if len(shards) > 0:
        values = shard_levels(own_key, dims, shards, -0.22, 0.18) * values
    return jnp.clip(values, min=-most, max=most).astype(kind)


def setup_inputs(seed: int = 0) -> dict:
    arg_keys = jax.random.split(jax.random.key(seed), 9)
    hidden = draw_hidden(jax.random.fold_in(arg_keys[8], 71), 0)
    norm_gain = jnp.clip(1.0 + 0.18 * jax.random.normal(arg_keys[1], (D,), jnp.float32), 0.1, 1.9)
    w_query = scatter_about(arg_keys[2], (D, HQ), D ** -0.5, 0.09375, ((1, 4),))
    w_out = scatter_about(arg_keys[3], (HQ, D), HQ ** -0.5, 0.09375, ((0, 4),))
    nb_keys = draw_nb_keys(jax.random.fold_in(arg_keys[8], 71), 0)
    nb_values = scatter_about(arg_keys[5], (NBLOCKS, NBR, HQ), 2.0, 10.0, ((0, 8), (2, 4)))
    neighbours = draw_neighbours(jax.random.fold_in(arg_keys[8], 71), 0)
    valid_spans = draw_valid_spans(jax.random.fold_in(arg_keys[8], 71), 0)
    return dict(hidden=hidden, norm_gain=norm_gain, w_query=w_query, w_out=w_out, nb_keys=nb_keys, nb_values=nb_values, neighbours=neighbours, valid_spans=valid_spans)


eps = 1e-05

def attend(query_rows, key_rows, value_rows):
    query_heads = query_rows.reshape(SPAN, HEADS, HS).astype(jnp.float32)
    key_heads = key_rows.reshape(2, NBR, HEADS, HS).astype(jnp.float32)
    value_heads = value_rows.reshape(2, NBR, HEADS, HS).astype(jnp.float32)
    factor = 1.0 / math.sqrt(HS)
    scores = jnp.einsum('qhd,nkhd->nqhk', query_heads, key_heads, precision=lax.Precision.HIGHEST) * factor
    score_top = lax.optimization_barrier(jnp.max(scores, axis=-1))
    weights = jnp.exp(scores - score_top[..., None])
    weight_sum = lax.optimization_barrier(jnp.sum(weights, axis=-1))
    rounded = lax.optimization_barrier(weights.astype(jnp.bfloat16)).astype(jnp.float32)
    summed = jnp.einsum('nqhk,nkhd->nqhd', rounded, value_heads, precision=lax.Precision.HIGHEST)
    part_out = lax.optimization_barrier((summed / weight_sum[..., None]).astype(jnp.bfloat16)).astype(jnp.float32)
    best_score = lax.optimization_barrier(jnp.max(score_top, axis=0))
    mix_weight = jnp.exp(score_top - best_score[None]) * weight_sum
    merged = lax.optimization_barrier(jnp.sum(part_out * mix_weight[..., None], axis=0)) / lax.optimization_barrier(jnp.sum(mix_weight, axis=0))[..., None]
    return merged.reshape(SPAN, HEADS * HS).astype(jnp.bfloat16)

def reference(hidden, norm_gain, w_query, w_out, nb_keys, nb_values, neighbours, valid_spans):
    widened = hidden.astype(jnp.float32)
    normed = (widened * lax.rsqrt(lax.optimization_barrier(jnp.mean(widened * widened, axis=1, keepdims=True)) + eps) * norm_gain).astype(jnp.bfloat16)
    queries = jnp.dot(normed, w_query, preferred_element_type=jnp.float32).astype(jnp.bfloat16)
    inner_width = HEADS * HS
    shifted = jnp.concatenate([queries[SPAN - 1:], jnp.zeros((SPAN - 1, inner_width), jnp.bfloat16)], axis=0)
    grouped = shifted.reshape(SPANS, SPAN, inner_width)

    def one_span(span_item):
        query_rows, block_ids = span_item
        return attend(query_rows, nb_keys[block_ids], nb_values[block_ids])
    attended = lax.map(one_span, (grouped, neighbours))
    span_order = jnp.arange(SPANS, dtype=jnp.int32)
    is_live = span_order % SPAN_DEV < valid_spans[span_order // SPAN_DEV]
    attended = jnp.where(is_live[:, None, None], attended, jnp.zeros_like(attended))
    flat_rows = attended.reshape(TOKENS, inner_width)
    placed = jnp.concatenate([jnp.zeros((SPAN - 1, inner_width), jnp.bfloat16), flat_rows[:TOKENS - SPAN + 1]], axis=0)
    return widened + jnp.dot(placed, w_out, preferred_element_type=jnp.float32)
```

```python
import functools
import math

import jax
import jax.numpy as jnp
from jax import lax
from jax.experimental import pallas as pl
from jax.experimental.pallas import tpu as pltpu
from jax.sharding import PartitionSpec as P

HS = 128
SPAN = 64
NBR = 128


eps = 1e-05


def shifted(block, axis, distance):
    devices = range(lax.axis_size(axis))
    route = [(i - distance, i) for i in devices if i - distance in devices]
    return lax.ppermute(block, axis, route)


def attention_kernel(slots, live, q_ref, k0_ref, k1_ref, v0_ref, v1_ref, out_ref):
    span = pl.program_id(0)
    factor = 1.0 / math.sqrt(HS)
    keep = live[span] > 0
    for head in range(q_ref.shape[1] // HS):
        cols = slice(head * HS, (head + 1) * HS)
        query = q_ref[:, cols]
        keys = jnp.concatenate([k0_ref[0, :, cols], k1_ref[0, :, cols]], axis=0)
        values = jnp.concatenate([v0_ref[0, :, cols], v1_ref[0, :, cols]], axis=0)
        scores = (
            lax.dot_general(
                query, keys, (((1,), (1,)), ((), ())), preferred_element_type=jnp.float32
            )
            * factor
        )
        weights = jnp.exp(scores - jnp.max(scores, axis=1, keepdims=True))
        total = jnp.sum(weights, axis=1, keepdims=True)
        summed = jnp.dot(
            weights.astype(jnp.bfloat16), values, preferred_element_type=jnp.float32
        )
        merged = summed / total
        out_ref[:, cols] = jnp.where(keep, merged, 0.0).astype(jnp.bfloat16)


def attention(slots, live, grouped, key_rows, value_rows):
    rows, width = grouped.shape
    spans = rows // SPAN

    def block(which):
        return pl.BlockSpec(
            (1, NBR, width), lambda span, slots, live: (slots[2 * span + which], 0, 0)
        )

    token_block = pl.BlockSpec((SPAN, width), lambda span, slots, live: (span, 0))
    return pl.pallas_call(
        attention_kernel,
        grid_spec=pltpu.PrefetchScalarGridSpec(
            num_scalar_prefetch=2,
            grid=(spans,),
            in_specs=[token_block, block(0), block(1), block(0), block(1)],
            out_specs=token_block,
        ),
        out_shape=jax.ShapeDtypeStruct((rows, width), jnp.bfloat16),
        compiler_params=pltpu.CompilerParams(vmem_limit_bytes=24 * 2**20),
        cost_estimate=pl.CostEstimate(
            flops=8 * rows * NBR * width,
            bytes_accessed=4 * rows * width + 8 * spans * NBR * width,
            transcendentals=2 * rows * NBR * width // HS,
        ),
    )(slots, live, grouped, key_rows, key_rows, value_rows, value_rows)


def shards(hidden, norm_gain, w_query, w_out, nb_keys, nb_values, neighbours, valid_spans):
    tok_rows = hidden.shape[0]
    span_dev = tok_rows // SPAN
    stored = nb_keys.shape[0]
    inner_width = w_query.shape[1]
    peer_count = lax.axis_size("dp")
    most_slots = max(2, (2 * span_dev + peer_count - 1) // peer_count)
    widened = lax.all_gather(hidden, "mp", axis=1, tiled=True).astype(jnp.float32)
    normed = (
        widened * lax.rsqrt(jnp.mean(widened * widened, axis=1, keepdims=True) + eps) * norm_gain
    ).astype(jnp.bfloat16)
    queries = jnp.dot(normed, w_query, preferred_element_type=jnp.float32).astype(jnp.bfloat16)
    following = shifted(queries[: SPAN - 1], "dp", -1)
    grouped = jnp.concatenate([queries[SPAN - 1 :], following], axis=0)
    live_span = jnp.arange(span_dev, dtype=jnp.int32) < valid_spans[0]
    owners = (neighbours // stored).reshape(-1)
    slot_ids = (neighbours % stored).reshape(-1)
    is_live = jnp.repeat(live_span, 2)
    req_order = jnp.arange(owners.shape[0], dtype=jnp.int32)
    earlier = (
        (owners[:, None] == owners[None, :])
        & is_live[None, :]
        & (req_order[None, :] < req_order[:, None])
    )
    slot_rank = jnp.minimum(jnp.sum(earlier.astype(jnp.int32), axis=1), most_slots - 1)
    target = jnp.where(is_live, owners * most_slots + slot_rank, -1)
    slot_match = target[:, None] == jnp.arange(peer_count * most_slots, dtype=jnp.int32)[None, :]
    filled = jnp.any(slot_match, axis=0)
    request_table = jnp.where(
        filled, jnp.sum(jnp.where(slot_match, slot_ids[:, None], 0), axis=0), -1
    )
    request_table = request_table.reshape(peer_count, most_slots)
    safe_ids = jnp.maximum(
        lax.all_to_all(request_table, "dp", split_axis=0, concat_axis=0, tiled=True), 0
    )
    keys_back = lax.all_to_all(nb_keys[safe_ids], "dp", split_axis=0, concat_axis=0, tiled=True)
    values_back = lax.all_to_all(nb_values[safe_ids], "dp", split_axis=0, concat_axis=0, tiled=True)
    flat_slots = (peer_count * most_slots, NBR, inner_width)
    merged = attention(
        owners * most_slots + slot_rank,
        live_span.astype(jnp.int32),
        grouped,
        keys_back.reshape(flat_slots),
        values_back.reshape(flat_slots),
    )
    previous = shifted(merged[tok_rows - SPAN + 1 :], "dp", 1)
    placed = jnp.concatenate([previous, merged[: tok_rows - SPAN + 1]], axis=0)
    head_terms = jnp.dot(placed, w_out, preferred_element_type=jnp.float32).astype(jnp.bfloat16)
    summed = lax.psum_scatter(head_terms, "mp", scatter_dimension=1, tiled=True)
    return hidden.astype(jnp.float32) + summed.astype(jnp.float32)


def solution(mesh):
    placed = (
        P("dp", "mp"),
        P(),
        P(None, "mp"),
        P("mp", None),
        P("dp", None, "mp"),
        P("dp", None, "mp"),
        P("dp", None),
        P("dp"),
    )
    return jax.shard_map(
        shards, mesh=mesh, in_specs=placed, out_specs=P("dp", "mp"), check_vma=False
    )
```

```python
import functools
import math

import jax
import jax.numpy as jnp
from jax import lax
from jax.experimental import pallas as pl
from jax.experimental.pallas import tpu as pltpu
from jax.sharding import PartitionSpec as P

HS = 128
SPAN = 64
NBR = 128


eps = 1e-05


def shifted(block, axis, distance):
    devices = range(lax.axis_size(axis))
    route = [(i - distance, i) for i in devices if i - distance in devices]
    return lax.ppermute(block, axis, route)


def attention_kernel(slots, live, q_ref, k0_ref, k1_ref, v0_ref, v1_ref, out_ref):
    span = pl.program_id(0)
    factor = 1.0 / math.sqrt(HS)
    keep = live[span] > 0
    for head in range(q_ref.shape[1] // HS):
        cols = slice(head * HS, (head + 1) * HS)
        query = q_ref[:, cols]
        keys = jnp.concatenate([k0_ref[0, :, cols], k1_ref[0, :, cols]], axis=0)
        values = jnp.concatenate([v0_ref[0, :, cols], v1_ref[0, :, cols]], axis=0)
        scores = (
            lax.dot_general(
                query, keys, (((1,), (1,)), ((), ())), preferred_element_type=jnp.float32
            )
            * factor
        )
        weights = jnp.exp(scores - jnp.max(scores, axis=1, keepdims=True))
        total = jnp.sum(weights, axis=1, keepdims=True)
        summed = jnp.dot(
            weights.astype(jnp.bfloat16), values, preferred_element_type=jnp.float32
        )
        merged = summed / total
        out_ref[:, cols] = jnp.where(keep, merged, 0.0).astype(jnp.bfloat16)


def attention(slots, live, grouped, key_rows, value_rows):
    rows, width = grouped.shape
    spans = rows // SPAN

    def block(which):
        return pl.BlockSpec(
            (1, NBR, width), lambda span, slots, live: (slots[2 * span + which], 0, 0)
        )

    token_block = pl.BlockSpec((SPAN, width), lambda span, slots, live: (span, 0))
    return pl.pallas_call(
        attention_kernel,
        grid_spec=pltpu.PrefetchScalarGridSpec(
            num_scalar_prefetch=2,
            grid=(spans,),
            in_specs=[token_block, block(0), block(1), block(0), block(1)],
            out_specs=token_block,
        ),
        out_shape=jax.ShapeDtypeStruct((rows, width), jnp.bfloat16),
        compiler_params=pltpu.CompilerParams(vmem_limit_bytes=24 * 2**20),
        cost_estimate=pl.CostEstimate(
            flops=8 * rows * NBR * width,
            bytes_accessed=4 * rows * width + 8 * spans * NBR * width,
            transcendentals=2 * rows * NBR * width // HS,
        ),
    )(slots, live, grouped, key_rows, key_rows, value_rows, value_rows)


def project_kernel(
    term_ref, w_ref, hidden_ref, out_ref, held, w_held, send_sem, recv_sem, w_sem
):
    me = lax.axis_index("mp")
    count = lax.axis_size("mp")
    width = hidden_ref.shape[1]
    chunks = held.shape[2]
    rows = held.shape[3]

    def fetch(dest):
        cols = pl.ds(pl.multiple_of(dest * width, width), width)
        return pltpu.make_async_copy(w_ref.at[:, cols], w_held.at[dest], w_sem.at[dest])

    for turn in range(count):
        fetch(count - 1 - turn // 2 if turn % 2 == 0 else turn // 2).start()

    barrier = pltpu.get_barrier_semaphore()

    @pl.when(me > 0)
    def _():
        pl.semaphore_signal(
            barrier, inc=1, device_id={"mp": me - 1}, device_id_type=pl.DeviceIdType.MESH
        )

    @pl.when(me < count - 1)
    def _():
        pl.semaphore_signal(
            barrier, inc=1, device_id={"mp": me + 1}, device_id_type=pl.DeviceIdType.MESH
        )

    has_both = jnp.logical_and(me > 0, me < count - 1)

    @pl.when(has_both)
    def _():
        pl.semaphore_wait(barrier, 2)

    @pl.when(jnp.logical_not(has_both))
    def _():
        pl.semaphore_wait(barrier, 1)

    def copy(way, turn, chunk, peer):
        return pltpu.make_async_remote_copy(
            src_ref=held.at[way, turn, chunk],
            dst_ref=held.at[way, turn, chunk],
            send_sem=send_sem.at[way, turn, chunk],
            recv_sem=recv_sem.at[way, turn, chunk],
            device_id={"mp": peer},
            device_id_type=pl.DeviceIdType.MESH,
        )

    def own(chunk, dest):
        first = pl.multiple_of(chunk * rows, rows)
        return jnp.dot(
            term_ref[pl.ds(first, rows), :], w_held[dest], preferred_element_type=jnp.float32
        )

    def pass_on(way, turn, chunk, dest, behind, ahead, has_behind):
        @pl.when(chunk == 0)
        def _():
            fetch(dest).wait()

        part = own(chunk, dest)

        @pl.when(has_behind)
        def _():
            copy(way, turn, chunk, behind).wait_recv()
            held[way, turn, chunk] = (
                part + held[way, turn, chunk].astype(jnp.float32)
            ).astype(jnp.bfloat16)

        @pl.when(jnp.logical_not(has_behind))
        def _():
            held[way, turn, chunk] = part.astype(jnp.bfloat16)

        copy(way, turn, chunk, ahead).start()

    def step(index, carry):
        turn = index // chunks
        chunk = index % chunks
        up = count - 1 - turn
        down = turn

        @pl.when(up > me)
        def _():
            pass_on(0, turn, chunk, up, me - 1, me + 1, me > 0)

        @pl.when(down < me)
        def _():
            pass_on(1, turn, chunk, down, me + 1, me - 1, me < count - 1)

        return carry

    lax.fori_loop(0, (count - 1) * chunks, step, 0)
    fetch(me).wait()

    def finish_own(chunk, carry):
        here = pl.ds(pl.multiple_of(chunk * rows, rows), rows)
        out_ref[here, :] = own(chunk, me) + hidden_ref[here, :].astype(jnp.float32)
        return carry

    lax.fori_loop(0, chunks, finish_own, 0)

    def finish(chunk, carry):
        here = pl.ds(pl.multiple_of(chunk * rows, rows), rows)

        @pl.when(me > 0)
        def _():
            copy(0, count - 1 - me, chunk, me - 1).wait_recv()
            out_ref[here, :] += held[0, count - 1 - me, chunk].astype(jnp.float32)

        @pl.when(me < count - 1)
        def _():
            copy(1, me, chunk, me + 1).wait_recv()
            out_ref[here, :] += held[1, me, chunk].astype(jnp.float32)

        return carry

    lax.fori_loop(0, chunks, finish, 0)

    def sent(index, carry):
        turn = index // chunks
        chunk = index % chunks

        @pl.when(count - 1 - turn > me)
        def _():
            copy(0, turn, chunk, me + 1).wait_send()

        @pl.when(turn < me)
        def _():
            copy(1, turn, chunk, me - 1).wait_send()

        return carry

    lax.fori_loop(0, (count - 1) * chunks, sent, 0)


def project(terms, w_out, hidden):
    tokens, width = hidden.shape
    inner = terms.shape[1]
    count = lax.axis_size("mp")
    chunks = 4
    rows = tokens // chunks
    vmem = pl.BlockSpec(memory_space=pltpu.VMEM)
    return pl.pallas_call(
        project_kernel,
        out_shape=jax.ShapeDtypeStruct((tokens, width), jnp.float32),
        in_specs=[vmem, pl.BlockSpec(memory_space=pl.ANY), vmem],
        out_specs=vmem,
        scratch_shapes=[
            pltpu.VMEM((2, count - 1, chunks, rows, width), jnp.bfloat16),
            pltpu.VMEM((count, inner, width), jnp.bfloat16),
            pltpu.SemaphoreType.DMA((2, count - 1, chunks)),
            pltpu.SemaphoreType.DMA((2, count - 1, chunks)),
            pltpu.SemaphoreType.DMA((count,)),
        ],
        compiler_params=pltpu.CompilerParams(
            collective_id=0, has_side_effects=True, vmem_limit_bytes=32 * 2**20
        ),
        cost_estimate=pl.CostEstimate(
            flops=2 * tokens * inner * width * count,
            bytes_accessed=2 * inner * width * count + 8 * tokens * width,
            transcendentals=0,
        ),
    )(terms, w_out, hidden)


def shards(hidden, norm_gain, w_query, w_out, nb_keys, nb_values, neighbours, valid_spans):
    tok_rows = hidden.shape[0]
    span_dev = tok_rows // SPAN
    stored = nb_keys.shape[0]
    inner_width = w_query.shape[1]
    peer_count = lax.axis_size("dp")
    most_slots = max(2, (2 * span_dev + peer_count - 1) // peer_count)
    widened = lax.all_gather(hidden, "mp", axis=1, tiled=True).astype(jnp.float32)
    normed = (
        widened * lax.rsqrt(jnp.mean(widened * widened, axis=1, keepdims=True) + eps) * norm_gain
    ).astype(jnp.bfloat16)
    queries = jnp.dot(normed, w_query, preferred_element_type=jnp.float32).astype(jnp.bfloat16)
    following = shifted(queries[: SPAN - 1], "dp", -1)
    grouped = jnp.concatenate([queries[SPAN - 1 :], following], axis=0)
    live_span = jnp.arange(span_dev, dtype=jnp.int32) < valid_spans[0]
    owners = (neighbours // stored).reshape(-1)
    slot_ids = (neighbours % stored).reshape(-1)
    is_live = jnp.repeat(live_span, 2)
    req_order = jnp.arange(owners.shape[0], dtype=jnp.int32)
    earlier = (
        (owners[:, None] == owners[None, :])
        & is_live[None, :]
        & (req_order[None, :] < req_order[:, None])
    )
    slot_rank = jnp.minimum(jnp.sum(earlier.astype(jnp.int32), axis=1), most_slots - 1)
    target = jnp.where(is_live, owners * most_slots + slot_rank, -1)
    slot_match = target[:, None] == jnp.arange(peer_count * most_slots, dtype=jnp.int32)[None, :]
    filled = jnp.any(slot_match, axis=0)
    request_table = jnp.where(
        filled, jnp.sum(jnp.where(slot_match, slot_ids[:, None], 0), axis=0), -1
    )
    request_table = request_table.reshape(peer_count, most_slots)
    safe_ids = jnp.maximum(
        lax.all_to_all(request_table, "dp", split_axis=0, concat_axis=0, tiled=True), 0
    )
    keys_back = lax.all_to_all(nb_keys[safe_ids], "dp", split_axis=0, concat_axis=0, tiled=True)
    values_back = lax.all_to_all(nb_values[safe_ids], "dp", split_axis=0, concat_axis=0, tiled=True)
    flat_slots = (peer_count * most_slots, NBR, inner_width)
    merged = attention(
        owners * most_slots + slot_rank,
        live_span.astype(jnp.int32),
        grouped,
        keys_back.reshape(flat_slots),
        values_back.reshape(flat_slots),
    )
    previous = shifted(merged[tok_rows - SPAN + 1 :], "dp", 1)
    placed = jnp.concatenate([previous, merged[: tok_rows - SPAN + 1]], axis=0)
    return project(placed, w_out, hidden)


def solution(mesh):
    placed = (
        P("dp", "mp"),
        P(),
        P(None, "mp"),
        P("mp", None),
        P("dp", None, "mp"),
        P("dp", None, "mp"),
        P("dp", None),
        P("dp"),
    )
    return jax.shard_map(
        shards, mesh=mesh, in_specs=placed, out_specs=P("dp", "mp"), check_vma=False
    )
```

```python
import functools
import math

import jax
import jax.numpy as jnp
from jax import lax
from jax.experimental import pallas as pl
from jax.experimental.pallas import tpu as pltpu
from jax.sharding import PartitionSpec as P

HS = 128
SPAN = 64
NBR = 128
DEPTH = 2


eps = 1e-05


def shifted(block, axis, distance):
    devices = range(lax.axis_size(axis))
    route = [(i - distance, i) for i in devices if i - distance in devices]
    return lax.ppermute(block, axis, route)


def attention_kernel(slots, live, q_ref, k0_ref, k1_ref, v0_ref, v1_ref, out_ref):
    span = pl.program_id(0)
    factor = 1.0 / math.sqrt(HS)
    keep = live[span] > 0
    for head in range(q_ref.shape[1] // HS):
        cols = slice(head * HS, (head + 1) * HS)
        query = q_ref[:, cols]
        keys = jnp.concatenate([k0_ref[0, :, cols], k1_ref[0, :, cols]], axis=0)
        values = jnp.concatenate([v0_ref[0, :, cols], v1_ref[0, :, cols]], axis=0)
        scores = (
            lax.dot_general(
                query, keys, (((1,), (1,)), ((), ())), preferred_element_type=jnp.float32
            )
            * factor
        )
        weights = jnp.exp(scores - jnp.max(scores, axis=1, keepdims=True))
        total = jnp.sum(weights, axis=1, keepdims=True)
        summed = jnp.dot(
            weights.astype(jnp.bfloat16), values, preferred_element_type=jnp.float32
        )
        merged = summed / total
        out_ref[:, cols] = jnp.where(keep, merged, 0.0).astype(jnp.bfloat16)


def attention(slots, live, grouped, key_rows, value_rows):
    rows, width = grouped.shape
    spans = rows // SPAN

    def block(which):
        return pl.BlockSpec(
            (1, NBR, width), lambda span, slots, live: (slots[2 * span + which], 0, 0)
        )

    token_block = pl.BlockSpec((SPAN, width), lambda span, slots, live: (span, 0))
    return pl.pallas_call(
        attention_kernel,
        grid_spec=pltpu.PrefetchScalarGridSpec(
            num_scalar_prefetch=2,
            grid=(spans,),
            in_specs=[token_block, block(0), block(1), block(0), block(1)],
            out_specs=token_block,
        ),
        out_shape=jax.ShapeDtypeStruct((rows, width), jnp.bfloat16),
        compiler_params=pltpu.CompilerParams(vmem_limit_bytes=24 * 2**20),
        cost_estimate=pl.CostEstimate(
            flops=8 * rows * NBR * width,
            bytes_accessed=4 * rows * width + 8 * spans * NBR * width,
            transcendentals=2 * rows * NBR * width // HS,
        ),
    )(slots, live, grouped, key_rows, key_rows, value_rows, value_rows)


def project_kernel(
    term_ref, w_ref, hidden_ref, out_ref, held, w_held, send_sem, recv_sem, w_sem
):
    me = lax.axis_index("mp")
    count = lax.axis_size("mp")
    width = hidden_ref.shape[1]
    chunks = held.shape[2]
    rows = held.shape[3]

    def fetch(dest):
        cols = pl.ds(pl.multiple_of(dest * width, width), width)
        return pltpu.make_async_copy(w_ref.at[:, cols], w_held.at[dest], w_sem.at[dest])

    for turn in range(count):
        fetch(count - 1 - turn // 2 if turn % 2 == 0 else turn // 2).start()

    barrier = pltpu.get_barrier_semaphore()

    @pl.when(me > 0)
    def _():
        pl.semaphore_signal(
            barrier, inc=1, device_id={"mp": me - 1}, device_id_type=pl.DeviceIdType.MESH
        )

    @pl.when(me < count - 1)
    def _():
        pl.semaphore_signal(
            barrier, inc=1, device_id={"mp": me + 1}, device_id_type=pl.DeviceIdType.MESH
        )

    has_both = jnp.logical_and(me > 0, me < count - 1)

    @pl.when(has_both)
    def _():
        pl.semaphore_wait(barrier, 2)

    @pl.when(jnp.logical_not(has_both))
    def _():
        pl.semaphore_wait(barrier, 1)

    def copy(way, turn, chunk, peer):
        return pltpu.make_async_remote_copy(
            src_ref=held.at[way, turn, chunk],
            dst_ref=held.at[way, turn, chunk],
            send_sem=send_sem.at[way, turn, chunk],
            recv_sem=recv_sem.at[way, turn, chunk],
            device_id={"mp": peer},
            device_id_type=pl.DeviceIdType.MESH,
        )

    def own(chunk, dest):
        first = pl.multiple_of(chunk * rows, rows)
        return jnp.dot(
            term_ref[pl.ds(first, rows), :], w_held[dest], preferred_element_type=jnp.float32
        )

    def pass_on(way, turn, chunk, dest, behind, ahead, has_behind):
        @pl.when(chunk == 0)
        def _():
            fetch(dest).wait()

        part = own(chunk, dest)

        @pl.when(has_behind)
        def _():
            copy(way, turn, chunk, behind).wait_recv()
            held[way, turn, chunk] = (
                part + held[way, turn, chunk].astype(jnp.float32)
            ).astype(jnp.bfloat16)

        @pl.when(jnp.logical_not(has_behind))
        def _():
            held[way, turn, chunk] = part.astype(jnp.bfloat16)

        before = turn * chunks + chunk - DEPTH

        @pl.when(before >= 0)
        def _():
            copy(way, before // chunks, before % chunks, ahead).wait_send()

        copy(way, turn, chunk, ahead).start()

    def step(index, carry):
        turn = index // chunks
        chunk = index % chunks
        up = count - 1 - turn
        down = turn

        @pl.when(up > me)
        def _():
            pass_on(0, turn, chunk, up, me - 1, me + 1, me > 0)

        @pl.when(down < me)
        def _():
            pass_on(1, turn, chunk, down, me + 1, me - 1, me < count - 1)

        return carry

    lax.fori_loop(0, (count - 1) * chunks, step, 0)
    fetch(me).wait()

    def finish_own(chunk, carry):
        here = pl.ds(pl.multiple_of(chunk * rows, rows), rows)
        out_ref[here, :] = own(chunk, me) + hidden_ref[here, :].astype(jnp.float32)
        return carry

    lax.fori_loop(0, chunks, finish_own, 0)

    def finish(chunk, carry):
        here = pl.ds(pl.multiple_of(chunk * rows, rows), rows)

        @pl.when(me > 0)
        def _():
            copy(0, count - 1 - me, chunk, me - 1).wait_recv()
            out_ref[here, :] += held[0, count - 1 - me, chunk].astype(jnp.float32)

        @pl.when(me < count - 1)
        def _():
            copy(1, me, chunk, me + 1).wait_recv()
            out_ref[here, :] += held[1, me, chunk].astype(jnp.float32)

        return carry

    lax.fori_loop(0, chunks, finish, 0)

    def sent(index, carry):
        turn = index // chunks
        chunk = index % chunks
        ups = (count - 1 - me) * chunks
        downs = me * chunks

        @pl.when(jnp.logical_and(index < ups, index >= ups - DEPTH))
        def _():
            copy(0, turn, chunk, me + 1).wait_send()

        @pl.when(jnp.logical_and(index < downs, index >= downs - DEPTH))
        def _():
            copy(1, turn, chunk, me - 1).wait_send()

        return carry

    lax.fori_loop(0, (count - 1) * chunks, sent, 0)


def project(terms, w_out, hidden):
    tokens, width = hidden.shape
    inner = terms.shape[1]
    count = lax.axis_size("mp")
    chunks = 4
    rows = tokens // chunks
    vmem = pl.BlockSpec(memory_space=pltpu.VMEM)
    return pl.pallas_call(
        project_kernel,
        out_shape=jax.ShapeDtypeStruct((tokens, width), jnp.float32),
        in_specs=[vmem, pl.BlockSpec(memory_space=pl.ANY), vmem],
        out_specs=vmem,
        scratch_shapes=[
            pltpu.VMEM((2, count - 1, chunks, rows, width), jnp.bfloat16),
            pltpu.VMEM((count, inner, width), jnp.bfloat16),
            pltpu.SemaphoreType.DMA((2, count - 1, chunks)),
            pltpu.SemaphoreType.DMA((2, count - 1, chunks)),
            pltpu.SemaphoreType.DMA((count,)),
        ],
        compiler_params=pltpu.CompilerParams(
            collective_id=0, has_side_effects=True, vmem_limit_bytes=56 * 2**20
        ),
        cost_estimate=pl.CostEstimate(
            flops=2 * tokens * inner * width * count,
            bytes_accessed=2 * inner * width * count + 8 * tokens * width,
            transcendentals=0,
        ),
    )(terms, w_out, hidden)


def shards(hidden, norm_gain, w_query, w_out, nb_keys, nb_values, neighbours, valid_spans):
    tok_rows = hidden.shape[0]
    span_dev = tok_rows // SPAN
    stored = nb_keys.shape[0]
    inner_width = w_query.shape[1]
    peer_count = lax.axis_size("dp")
    most_slots = max(2, (2 * span_dev + peer_count - 1) // peer_count)
    following = shifted(hidden[: SPAN - 1], "dp", -1)
    attending = jnp.concatenate([hidden[SPAN - 1 :], following], axis=0)
    widened = lax.all_gather(attending, "mp", axis=1, tiled=True).astype(jnp.float32)
    normed = (
        widened * lax.rsqrt(jnp.mean(widened * widened, axis=1, keepdims=True) + eps) * norm_gain
    ).astype(jnp.bfloat16)
    grouped = jnp.dot(normed, w_query, preferred_element_type=jnp.float32).astype(jnp.bfloat16)
    live_span = jnp.arange(span_dev, dtype=jnp.int32) < valid_spans[0]
    owners = (neighbours // stored).reshape(-1)
    slot_ids = (neighbours % stored).reshape(-1)
    is_live = jnp.repeat(live_span, 2)
    req_order = jnp.arange(owners.shape[0], dtype=jnp.int32)
    earlier = (
        (owners[:, None] == owners[None, :])
        & is_live[None, :]
        & (req_order[None, :] < req_order[:, None])
    )
    slot_rank = jnp.minimum(jnp.sum(earlier.astype(jnp.int32), axis=1), most_slots - 1)
    target = jnp.where(is_live, owners * most_slots + slot_rank, -1)
    slot_match = target[:, None] == jnp.arange(peer_count * most_slots, dtype=jnp.int32)[None, :]
    filled = jnp.any(slot_match, axis=0)
    request_table = jnp.where(
        filled, jnp.sum(jnp.where(slot_match, slot_ids[:, None], 0), axis=0), -1
    )
    request_table = request_table.reshape(peer_count, most_slots)
    safe_ids = jnp.maximum(
        lax.all_to_all(request_table, "dp", split_axis=0, concat_axis=0, tiled=True), 0
    )
    keys_back = lax.all_to_all(nb_keys[safe_ids], "dp", split_axis=0, concat_axis=0, tiled=True)
    values_back = lax.all_to_all(nb_values[safe_ids], "dp", split_axis=0, concat_axis=0, tiled=True)
    flat_slots = (peer_count * most_slots, NBR, inner_width)
    merged = attention(
        owners * most_slots + slot_rank,
        live_span.astype(jnp.int32),
        grouped,
        keys_back.reshape(flat_slots),
        values_back.reshape(flat_slots),
    )
    previous = shifted(merged[tok_rows - SPAN + 1 :], "dp", 1)
    placed = jnp.concatenate([previous, merged[: tok_rows - SPAN + 1]], axis=0)
    return project(placed, w_out, hidden)


def solution(mesh):
    placed = (
        P("dp", "mp"),
        P(),
        P(None, "mp"),
        P("mp", None),
        P("dp", None, "mp"),
        P("dp", None, "mp"),
        P("dp", None),
        P("dp"),
    )
    return jax.shard_map(
        shards, mesh=mesh, in_specs=placed, out_specs=P("dp", "mp"), check_vma=False
    )
```

```python
import functools
import math

import jax
import jax.numpy as jnp
from jax import lax
from jax.experimental import pallas as pl
from jax.experimental.pallas import tpu as pltpu
from jax.sharding import PartitionSpec as P

HS = 128
SPAN = 64
NBR = 128
DEPTH = 3


eps = 1e-05


def shifted(block, axis, distance):
    devices = range(lax.axis_size(axis))
    route = [(i - distance, i) for i in devices if i - distance in devices]
    return lax.ppermute(block, axis, route)


def attention_kernel(slots, live, q_ref, k0_ref, k1_ref, v0_ref, v1_ref, out_ref):
    span = pl.program_id(0)
    factor = 1.0 / math.sqrt(HS)
    keep = live[span] > 0
    for head in range(q_ref.shape[1] // HS):
        cols = slice(head * HS, (head + 1) * HS)
        query = q_ref[:, cols]
        keys = jnp.concatenate([k0_ref[0, :, cols], k1_ref[0, :, cols]], axis=0)
        values = jnp.concatenate([v0_ref[0, :, cols], v1_ref[0, :, cols]], axis=0)
        scores = (
            lax.dot_general(
                query, keys, (((1,), (1,)), ((), ())), preferred_element_type=jnp.float32
            )
            * factor
        )
        weights = jnp.exp(scores - jnp.max(scores, axis=1, keepdims=True))
        total = jnp.sum(weights, axis=1, keepdims=True)
        summed = jnp.dot(
            weights.astype(jnp.bfloat16), values, preferred_element_type=jnp.float32
        )
        merged = summed / total
        out_ref[:, cols] = jnp.where(keep, merged, 0.0).astype(jnp.bfloat16)


def attention(slots, live, grouped, key_rows, value_rows):
    rows, width = grouped.shape
    spans = rows // SPAN

    def block(which):
        return pl.BlockSpec(
            (1, NBR, width), lambda span, slots, live: (slots[2 * span + which], 0, 0)
        )

    token_block = pl.BlockSpec((SPAN, width), lambda span, slots, live: (span, 0))
    return pl.pallas_call(
        attention_kernel,
        grid_spec=pltpu.PrefetchScalarGridSpec(
            num_scalar_prefetch=2,
            grid=(spans,),
            in_specs=[token_block, block(0), block(1), block(0), block(1)],
            out_specs=token_block,
        ),
        out_shape=jax.ShapeDtypeStruct((rows, width), jnp.bfloat16),
        compiler_params=pltpu.CompilerParams(vmem_limit_bytes=24 * 2**20),
        cost_estimate=pl.CostEstimate(
            flops=8 * rows * NBR * width,
            bytes_accessed=4 * rows * width + 8 * spans * NBR * width,
            transcendentals=2 * rows * NBR * width // HS,
        ),
    )(slots, live, grouped, key_rows, key_rows, value_rows, value_rows)


def project_kernel(
    term_ref, w_ref, hidden_ref, out_ref, held, w_held, send_sem, recv_sem, w_sem
):
    me = lax.axis_index("mp")
    count = lax.axis_size("mp")
    width = hidden_ref.shape[1]
    chunks = held.shape[2]
    rows = held.shape[3]

    def fetch(dest):
        cols = pl.ds(pl.multiple_of(dest * width, width), width)
        return pltpu.make_async_copy(w_ref.at[:, cols], w_held.at[dest], w_sem.at[dest])

    for turn in range(count):
        fetch(count - 1 - turn // 2 if turn % 2 == 0 else turn // 2).start()

    barrier = pltpu.get_barrier_semaphore()

    @pl.when(me > 0)
    def _():
        pl.semaphore_signal(
            barrier, inc=1, device_id={"mp": me - 1}, device_id_type=pl.DeviceIdType.MESH
        )

    @pl.when(me < count - 1)
    def _():
        pl.semaphore_signal(
            barrier, inc=1, device_id={"mp": me + 1}, device_id_type=pl.DeviceIdType.MESH
        )

    has_both = jnp.logical_and(me > 0, me < count - 1)

    @pl.when(has_both)
    def _():
        pl.semaphore_wait(barrier, 2)

    @pl.when(jnp.logical_not(has_both))
    def _():
        pl.semaphore_wait(barrier, 1)

    def copy(way, turn, chunk, peer):
        return pltpu.make_async_remote_copy(
            src_ref=held.at[way, turn, chunk],
            dst_ref=held.at[way, turn, chunk],
            send_sem=send_sem.at[way, turn, chunk],
            recv_sem=recv_sem.at[way, turn, chunk],
            device_id={"mp": peer},
            device_id_type=pl.DeviceIdType.MESH,
        )

    def own(chunk, dest):
        first = pl.multiple_of(chunk * rows, rows)
        return jnp.dot(
            term_ref[pl.ds(first, rows), :], w_held[dest], preferred_element_type=jnp.float32
        )

    def pass_on(way, turn, chunk, dest, behind, ahead, has_behind):
        @pl.when(chunk == 0)
        def _():
            fetch(dest).wait()

        part = own(chunk, dest)

        @pl.when(has_behind)
        def _():
            copy(way, turn, chunk, behind).wait_recv()
            held[way, turn, chunk] = (
                part + held[way, turn, chunk].astype(jnp.float32)
            ).astype(jnp.bfloat16)

        @pl.when(jnp.logical_not(has_behind))
        def _():
            held[way, turn, chunk] = part.astype(jnp.bfloat16)

        before = turn * chunks + chunk - DEPTH

        @pl.when(before >= 0)
        def _():
            copy(way, before // chunks, before % chunks, ahead).wait_send()

        copy(way, turn, chunk, ahead).start()

    def step(tick, carry):
        up_index = tick - me
        down_index = tick - (count - 1 - me)

        @pl.when(jnp.logical_and(up_index >= 0, up_index < (count - 1 - me) * chunks))
        def _():
            turn = up_index // chunks
            pass_on(
                0, turn, up_index % chunks, count - 1 - turn, me - 1, me + 1, me > 0
            )

        @pl.when(jnp.logical_and(down_index >= 0, down_index < me * chunks))
        def _():
            turn = down_index // chunks
            pass_on(1, turn, down_index % chunks, turn, me + 1, me - 1, me < count - 1)

        return carry

    lax.fori_loop(0, (count - 1) * chunks, step, 0)
    fetch(me).wait()

    def finish_own(chunk, carry):
        here = pl.ds(pl.multiple_of(chunk * rows, rows), rows)
        out_ref[here, :] = own(chunk, me) + hidden_ref[here, :].astype(jnp.float32)
        return carry

    lax.fori_loop(0, chunks, finish_own, 0)

    def finish(chunk, carry):
        here = pl.ds(pl.multiple_of(chunk * rows, rows), rows)

        @pl.when(me > 0)
        def _():
            copy(0, count - 1 - me, chunk, me - 1).wait_recv()
            out_ref[here, :] += held[0, count - 1 - me, chunk].astype(jnp.float32)

        @pl.when(me < count - 1)
        def _():
            copy(1, me, chunk, me + 1).wait_recv()
            out_ref[here, :] += held[1, me, chunk].astype(jnp.float32)

        return carry

    lax.fori_loop(0, chunks, finish, 0)

    def sent(index, carry):
        turn = index // chunks
        chunk = index % chunks
        ups = (count - 1 - me) * chunks
        downs = me * chunks

        @pl.when(jnp.logical_and(index < ups, index >= ups - DEPTH))
        def _():
            copy(0, turn, chunk, me + 1).wait_send()

        @pl.when(jnp.logical_and(index < downs, index >= downs - DEPTH))
        def _():
            copy(1, turn, chunk, me - 1).wait_send()

        return carry

    lax.fori_loop(0, (count - 1) * chunks, sent, 0)


def project(terms, w_out, hidden):
    tokens, width = hidden.shape
    inner = terms.shape[1]
    count = lax.axis_size("mp")
    chunks = 4
    rows = tokens // chunks
    vmem = pl.BlockSpec(memory_space=pltpu.VMEM)
    return pl.pallas_call(
        project_kernel,
        out_shape=jax.ShapeDtypeStruct((tokens, width), jnp.float32),
        in_specs=[vmem, pl.BlockSpec(memory_space=pl.ANY), vmem],
        out_specs=vmem,
        scratch_shapes=[
            pltpu.VMEM((2, count - 1, chunks, rows, width), jnp.bfloat16),
            pltpu.VMEM((count, inner, width), jnp.bfloat16),
            pltpu.SemaphoreType.DMA((2, count - 1, chunks)),
            pltpu.SemaphoreType.DMA((2, count - 1, chunks)),
            pltpu.SemaphoreType.DMA((count,)),
        ],
        compiler_params=pltpu.CompilerParams(
            collective_id=0, has_side_effects=True, vmem_limit_bytes=56 * 2**20
        ),
        cost_estimate=pl.CostEstimate(
            flops=2 * tokens * inner * width * count,
            bytes_accessed=2 * inner * width * count + 8 * tokens * width,
            transcendentals=0,
        ),
    )(terms, w_out, hidden)


def shards(hidden, norm_gain, w_query, w_out, nb_keys, nb_values, neighbours, valid_spans):
    tok_rows = hidden.shape[0]
    span_dev = tok_rows // SPAN
    stored = nb_keys.shape[0]
    inner_width = w_query.shape[1]
    peer_count = lax.axis_size("dp")
    most_slots = max(2, (2 * span_dev + peer_count - 1) // peer_count)
    widened = lax.all_gather(hidden, "mp", axis=1, tiled=True).astype(jnp.float32)
    normed = (
        widened * lax.rsqrt(jnp.mean(widened * widened, axis=1, keepdims=True) + eps) * norm_gain
    ).astype(jnp.bfloat16)
    queries = jnp.dot(normed, w_query, preferred_element_type=jnp.float32).astype(jnp.bfloat16)
    following = shifted(queries[: SPAN - 1], "dp", -1)
    grouped = jnp.concatenate([queries[SPAN - 1 :], following], axis=0)
    live_span = jnp.arange(span_dev, dtype=jnp.int32) < valid_spans[0]
    owners = (neighbours // stored).reshape(-1)
    slot_ids = (neighbours % stored).reshape(-1)
    is_live = jnp.repeat(live_span, 2)
    req_order = jnp.arange(owners.shape[0], dtype=jnp.int32)
    earlier = (
        (owners[:, None] == owners[None, :])
        & is_live[None, :]
        & (req_order[None, :] < req_order[:, None])
    )
    slot_rank = jnp.minimum(jnp.sum(earlier.astype(jnp.int32), axis=1), most_slots - 1)
    target = jnp.where(is_live, owners * most_slots + slot_rank, -1)
    slot_match = target[:, None] == jnp.arange(peer_count * most_slots, dtype=jnp.int32)[None, :]
    filled = jnp.any(slot_match, axis=0)
    request_table = jnp.where(
        filled, jnp.sum(jnp.where(slot_match, slot_ids[:, None], 0), axis=0), -1
    )
    request_table = request_table.reshape(peer_count, most_slots)
    safe_ids = jnp.maximum(
        lax.all_to_all(request_table, "dp", split_axis=0, concat_axis=0, tiled=True), 0
    )
    keys_back = lax.all_to_all(nb_keys[safe_ids], "dp", split_axis=0, concat_axis=0, tiled=True)
    values_back = lax.all_to_all(nb_values[safe_ids], "dp", split_axis=0, concat_axis=0, tiled=True)
    flat_slots = (peer_count * most_slots, NBR, inner_width)
    merged = attention(
        owners * most_slots + slot_rank,
        live_span.astype(jnp.int32),
        grouped,
        keys_back.reshape(flat_slots),
        values_back.reshape(flat_slots),
    )
    previous = shifted(merged[tok_rows - SPAN + 1 :], "dp", 1)
    placed = jnp.concatenate([previous, merged[: tok_rows - SPAN + 1]], axis=0)
    return project(placed, w_out, hidden)


def solution(mesh):
    placed = (
        P("dp", "mp"),
        P(),
        P(None, "mp"),
        P("mp", None),
        P("dp", None, "mp"),
        P("dp", None, "mp"),
        P("dp", None),
        P("dp"),
    )
    return jax.shard_map(
        shards, mesh=mesh, in_specs=placed, out_specs=P("dp", "mp"), check_vma=False
    )
```

```python
import functools
import math

import jax
import jax.numpy as jnp
from jax import lax
from jax.experimental import pallas as pl
from jax.experimental.pallas import tpu as pltpu
from jax.sharding import PartitionSpec as P

HS = 128
SPAN = 64
NBR = 128
DEPTH = 3


eps = 1e-05


def shifted(block, axis, distance):
    devices = range(lax.axis_size(axis))
    route = [(i - distance, i) for i in devices if i - distance in devices]
    return lax.ppermute(block, axis, route)


def attention_kernel(slots, live, q_ref, k0_ref, k1_ref, v0_ref, v1_ref, out_ref):
    span = pl.program_id(0)
    factor = 1.0 / math.sqrt(HS)
    keep = live[span] > 0
    for head in range(q_ref.shape[1] // HS):
        cols = slice(head * HS, (head + 1) * HS)
        query = q_ref[:, cols]
        keys = jnp.concatenate([k0_ref[0, :, cols], k1_ref[0, :, cols]], axis=0)
        values = jnp.concatenate([v0_ref[0, :, cols], v1_ref[0, :, cols]], axis=0)
        scores = (
            lax.dot_general(
                query, keys, (((1,), (1,)), ((), ())), preferred_element_type=jnp.float32
            )
            * factor
        )
        weights = jnp.exp(scores - jnp.max(scores, axis=1, keepdims=True))
        total = jnp.sum(weights, axis=1, keepdims=True)
        summed = jnp.dot(
            weights.astype(jnp.bfloat16), values, preferred_element_type=jnp.float32
        )
        merged = summed / total
        out_ref[:, cols] = jnp.where(keep, merged, 0.0).astype(jnp.bfloat16)


def attention(slots, live, grouped, key_rows, value_rows):
    rows, width = grouped.shape
    spans = rows // SPAN

    def block(which):
        return pl.BlockSpec(
            (1, NBR, width), lambda span, slots, live: (slots[2 * span + which], 0, 0)
        )

    token_block = pl.BlockSpec((SPAN, width), lambda span, slots, live: (span, 0))
    return pl.pallas_call(
        attention_kernel,
        grid_spec=pltpu.PrefetchScalarGridSpec(
            num_scalar_prefetch=2,
            grid=(spans,),
            in_specs=[token_block, block(0), block(1), block(0), block(1)],
            out_specs=token_block,
        ),
        out_shape=jax.ShapeDtypeStruct((rows, width), jnp.bfloat16),
        compiler_params=pltpu.CompilerParams(vmem_limit_bytes=24 * 2**20),
        cost_estimate=pl.CostEstimate(
            flops=8 * rows * NBR * width,
            bytes_accessed=4 * rows * width + 8 * spans * NBR * width,
            transcendentals=2 * rows * NBR * width // HS,
        ),
    )(slots, live, grouped, key_rows, key_rows, value_rows, value_rows)


def weights_kernel(slots, q_ref, k0_ref, k1_ref, out_ref):
    factor = 1.0 / math.sqrt(HS)
    for head in range(q_ref.shape[1] // HS):
        cols = slice(head * HS, (head + 1) * HS)
        keys = jnp.concatenate([k0_ref[0, :, cols], k1_ref[0, :, cols]], axis=0)
        scores = (
            lax.dot_general(
                q_ref[:, cols],
                keys,
                (((1,), (1,)), ((), ())),
                preferred_element_type=jnp.float32,
            )
            * factor
        )
        weights = jnp.exp(scores - jnp.max(scores, axis=1, keepdims=True))
        total = jnp.sum(weights, axis=1, keepdims=True)
        place = slice(head * 2 * NBR, (head + 1) * 2 * NBR)
        out_ref[:, place] = (weights * (1.0 / total)).astype(jnp.bfloat16)


def values_kernel(slots, live, weights_ref, v0_ref, v1_ref, out_ref):
    keep = live[pl.program_id(0)] > 0
    for head in range(out_ref.shape[1] // HS):
        cols = slice(head * HS, (head + 1) * HS)
        values = jnp.concatenate([v0_ref[0, :, cols], v1_ref[0, :, cols]], axis=0)
        place = slice(head * 2 * NBR, (head + 1) * 2 * NBR)
        merged = jnp.dot(weights_ref[:, place], values, preferred_element_type=jnp.float32)
        out_ref[:, cols] = jnp.where(keep, merged, 0.0).astype(jnp.bfloat16)


def weigh(slots, queries, key_rows):
    rows, width = queries.shape
    spans = rows // SPAN
    spread = width // HS * 2 * NBR

    def block(which):
        return pl.BlockSpec((1, NBR, width), lambda span, slots: (slots[2 * span + which], 0, 0))

    return pl.pallas_call(
        weights_kernel,
        grid_spec=pltpu.PrefetchScalarGridSpec(
            num_scalar_prefetch=1,
            grid=(spans,),
            in_specs=[
                pl.BlockSpec((SPAN, width), lambda span, slots: (span, 0)),
                block(0),
                block(1),
            ],
            out_specs=pl.BlockSpec((SPAN, spread), lambda span, slots: (span, 0)),
        ),
        out_shape=jax.ShapeDtypeStruct((rows, spread), jnp.bfloat16),
        compiler_params=pltpu.CompilerParams(vmem_limit_bytes=24 * 2**20),
        cost_estimate=pl.CostEstimate(
            flops=4 * rows * NBR * width,
            bytes_accessed=2 * rows * width + 4 * spans * NBR * width + 2 * rows * spread,
            transcendentals=rows * spread,
        ),
    )(slots, queries, key_rows, key_rows)


def combine(slots, live, weights, value_rows):
    rows, spread = weights.shape
    spans = rows // SPAN
    width = value_rows.shape[2]

    def block(which):
        return pl.BlockSpec(
            (1, NBR, width), lambda span, slots, live: (slots[2 * span + which], 0, 0)
        )

    return pl.pallas_call(
        values_kernel,
        grid_spec=pltpu.PrefetchScalarGridSpec(
            num_scalar_prefetch=2,
            grid=(spans,),
            in_specs=[
                pl.BlockSpec((SPAN, spread), lambda span, slots, live: (span, 0)),
                block(0),
                block(1),
            ],
            out_specs=pl.BlockSpec((SPAN, width), lambda span, slots, live: (span, 0)),
        ),
        out_shape=jax.ShapeDtypeStruct((rows, width), jnp.bfloat16),
        compiler_params=pltpu.CompilerParams(vmem_limit_bytes=24 * 2**20),
        cost_estimate=pl.CostEstimate(
            flops=4 * rows * NBR * width,
            bytes_accessed=2 * rows * width + 4 * spans * NBR * width + 2 * rows * spread,
            transcendentals=0,
        ),
    )(slots, live, weights, value_rows, value_rows)


def project_kernel(
    term_ref, w_ref, hidden_ref, out_ref, held, w_held, send_sem, recv_sem, w_sem
):
    me = lax.axis_index("mp")
    count = lax.axis_size("mp")
    width = hidden_ref.shape[1]
    chunks = held.shape[2]
    rows = held.shape[3]

    def fetch(dest):
        cols = pl.ds(pl.multiple_of(dest * width, width), width)
        return pltpu.make_async_copy(w_ref.at[:, cols], w_held.at[dest], w_sem.at[dest])

    for turn in range(count):
        fetch(count - 1 - turn // 2 if turn % 2 == 0 else turn // 2).start()

    barrier = pltpu.get_barrier_semaphore()

    @pl.when(me > 0)
    def _():
        pl.semaphore_signal(
            barrier, inc=1, device_id={"mp": me - 1}, device_id_type=pl.DeviceIdType.MESH
        )

    @pl.when(me < count - 1)
    def _():
        pl.semaphore_signal(
            barrier, inc=1, device_id={"mp": me + 1}, device_id_type=pl.DeviceIdType.MESH
        )

    has_both = jnp.logical_and(me > 0, me < count - 1)

    @pl.when(has_both)
    def _():
        pl.semaphore_wait(barrier, 2)

    @pl.when(jnp.logical_not(has_both))
    def _():
        pl.semaphore_wait(barrier, 1)

    def copy(way, turn, chunk, peer):
        return pltpu.make_async_remote_copy(
            src_ref=held.at[way, turn, chunk],
            dst_ref=held.at[way, turn, chunk],
            send_sem=send_sem.at[way, turn, chunk],
            recv_sem=recv_sem.at[way, turn, chunk],
            device_id={"mp": peer},
            device_id_type=pl.DeviceIdType.MESH,
        )

    def own(chunk, dest):
        first = pl.multiple_of(chunk * rows, rows)
        return jnp.dot(
            term_ref[pl.ds(first, rows), :], w_held[dest], preferred_element_type=jnp.float32
        )

    def pass_on(way, turn, chunk, dest, behind, ahead, has_behind):
        @pl.when(chunk == 0)
        def _():
            fetch(dest).wait()

        part = own(chunk, dest)

        @pl.when(has_behind)
        def _():
            copy(way, turn, chunk, behind).wait_recv()
            held[way, turn, chunk] = (
                part + held[way, turn, chunk].astype(jnp.float32)
            ).astype(jnp.bfloat16)

        @pl.when(jnp.logical_not(has_behind))
        def _():
            held[way, turn, chunk] = part.astype(jnp.bfloat16)

        before = turn * chunks + chunk - DEPTH

        @pl.when(before >= 0)
        def _():
            copy(way, before // chunks, before % chunks, ahead).wait_send()

        copy(way, turn, chunk, ahead).start()

    def step(tick, carry):
        up_index = tick - me
        down_index = tick - (count - 1 - me)

        @pl.when(jnp.logical_and(up_index >= 0, up_index < (count - 1 - me) * chunks))
        def _():
            turn = up_index // chunks
            pass_on(
                0, turn, up_index % chunks, count - 1 - turn, me - 1, me + 1, me > 0
            )

        @pl.when(jnp.logical_and(down_index >= 0, down_index < me * chunks))
        def _():
            turn = down_index // chunks
            pass_on(1, turn, down_index % chunks, turn, me + 1, me - 1, me < count - 1)

        return carry

    lax.fori_loop(0, (count - 1) * chunks, step, 0)
    fetch(me).wait()

    def finish_own(chunk, carry):
        here = pl.ds(pl.multiple_of(chunk * rows, rows), rows)
        out_ref[here, :] = own(chunk, me) + hidden_ref[here, :].astype(jnp.float32)
        return carry

    lax.fori_loop(0, chunks, finish_own, 0)

    def finish(chunk, carry):
        here = pl.ds(pl.multiple_of(chunk * rows, rows), rows)

        @pl.when(me > 0)
        def _():
            copy(0, count - 1 - me, chunk, me - 1).wait_recv()
            out_ref[here, :] += held[0, count - 1 - me, chunk].astype(jnp.float32)

        @pl.when(me < count - 1)
        def _():
            copy(1, me, chunk, me + 1).wait_recv()
            out_ref[here, :] += held[1, me, chunk].astype(jnp.float32)

        return carry

    lax.fori_loop(0, chunks, finish, 0)

    def sent(index, carry):
        turn = index // chunks
        chunk = index % chunks
        ups = (count - 1 - me) * chunks
        downs = me * chunks

        @pl.when(jnp.logical_and(index < ups, index >= ups - DEPTH))
        def _():
            copy(0, turn, chunk, me + 1).wait_send()

        @pl.when(jnp.logical_and(index < downs, index >= downs - DEPTH))
        def _():
            copy(1, turn, chunk, me - 1).wait_send()

        return carry

    lax.fori_loop(0, (count - 1) * chunks, sent, 0)


def project(terms, w_out, hidden):
    tokens, width = hidden.shape
    inner = terms.shape[1]
    count = lax.axis_size("mp")
    chunks = 4
    rows = tokens // chunks
    vmem = pl.BlockSpec(memory_space=pltpu.VMEM)
    return pl.pallas_call(
        project_kernel,
        out_shape=jax.ShapeDtypeStruct((tokens, width), jnp.float32),
        in_specs=[vmem, pl.BlockSpec(memory_space=pl.ANY), vmem],
        out_specs=vmem,
        scratch_shapes=[
            pltpu.VMEM((2, count - 1, chunks, rows, width), jnp.bfloat16),
            pltpu.VMEM((count, inner, width), jnp.bfloat16),
            pltpu.SemaphoreType.DMA((2, count - 1, chunks)),
            pltpu.SemaphoreType.DMA((2, count - 1, chunks)),
            pltpu.SemaphoreType.DMA((count,)),
        ],
        compiler_params=pltpu.CompilerParams(
            collective_id=0, has_side_effects=True, vmem_limit_bytes=56 * 2**20
        ),
        cost_estimate=pl.CostEstimate(
            flops=2 * tokens * inner * width * count,
            bytes_accessed=2 * inner * width * count + 8 * tokens * width,
            transcendentals=0,
        ),
    )(terms, w_out, hidden)


def shards(hidden, norm_gain, w_query, w_out, nb_keys, nb_values, neighbours, valid_spans):
    tok_rows = hidden.shape[0]
    span_dev = tok_rows // SPAN
    stored = nb_keys.shape[0]
    inner_width = w_query.shape[1]
    peer_count = lax.axis_size("dp")
    most_slots = max(2, (2 * span_dev + peer_count - 1) // peer_count)
    widened = lax.all_gather(hidden, "mp", axis=1, tiled=True).astype(jnp.float32)
    normed = (
        widened * lax.rsqrt(jnp.mean(widened * widened, axis=1, keepdims=True) + eps) * norm_gain
    ).astype(jnp.bfloat16)
    queries = jnp.dot(normed, w_query, preferred_element_type=jnp.float32).astype(jnp.bfloat16)
    following = shifted(queries[: SPAN - 1], "dp", -1)
    inside = queries[SPAN - 1 : tok_rows - 1]
    crossing = jnp.concatenate([queries[tok_rows - 1 :], following], axis=0)
    live_span = jnp.arange(span_dev, dtype=jnp.int32) < valid_spans[0]
    owners = (neighbours // stored).reshape(-1)
    slot_ids = (neighbours % stored).reshape(-1)
    is_live = jnp.repeat(live_span, 2)
    req_order = jnp.arange(owners.shape[0], dtype=jnp.int32)
    earlier = (
        (owners[:, None] == owners[None, :])
        & is_live[None, :]
        & (req_order[None, :] < req_order[:, None])
    )
    slot_rank = jnp.minimum(jnp.sum(earlier.astype(jnp.int32), axis=1), most_slots - 1)
    target = jnp.where(is_live, owners * most_slots + slot_rank, -1)
    slot_match = target[:, None] == jnp.arange(peer_count * most_slots, dtype=jnp.int32)[None, :]
    filled = jnp.any(slot_match, axis=0)
    request_table = jnp.where(
        filled, jnp.sum(jnp.where(slot_match, slot_ids[:, None], 0), axis=0), -1
    )
    request_table = request_table.reshape(peer_count, most_slots)
    safe_ids = jnp.maximum(
        lax.all_to_all(request_table, "dp", split_axis=0, concat_axis=0, tiled=True), 0
    )
    keys_back = lax.all_to_all(nb_keys[safe_ids], "dp", split_axis=0, concat_axis=0, tiled=True)
    values_back = lax.all_to_all(nb_values[safe_ids], "dp", split_axis=0, concat_axis=0, tiled=True)
    flat_slots = (peer_count * most_slots, NBR, inner_width)
    key_rows = keys_back.reshape(flat_slots)
    value_rows = values_back.reshape(flat_slots)
    slots = owners * most_slots + slot_rank
    live = live_span.astype(jnp.int32)
    split = 2 * (span_dev - 1)
    weights = weigh(slots[:split], inside, key_rows)
    last = attention(slots[split:], live[span_dev - 1 :], crossing, key_rows, value_rows)
    previous = shifted(last[1:], "dp", 1)
    merged = combine(slots[:split], live[: span_dev - 1], weights, value_rows)
    placed = jnp.concatenate([previous, merged, last[:1]], axis=0)
    return project(placed, w_out, hidden)


def solution(mesh):
    placed = (
        P("dp", "mp"),
        P(),
        P(None, "mp"),
        P("mp", None),
        P("dp", None, "mp"),
        P("dp", None, "mp"),
        P("dp", None),
        P("dp"),
    )
    return jax.shard_map(
        shards, mesh=mesh, in_specs=placed, out_specs=P("dp", "mp"), check_vma=False
    )
```

```python
import functools
import math

import jax
import jax.numpy as jnp
from jax import lax
from jax.experimental import pallas as pl
from jax.experimental.pallas import tpu as pltpu
from jax.sharding import PartitionSpec as P

HS = 128
SPAN = 64
NBR = 128
DEPTH = 3


eps = 1e-05


def shifted(block, axis, distance):
    devices = range(lax.axis_size(axis))
    route = [(i - distance, i) for i in devices if i - distance in devices]
    return lax.ppermute(block, axis, route)


def attention_kernel(slots, live, q_ref, k0_ref, k1_ref, v0_ref, v1_ref, out_ref):
    span = pl.program_id(0)
    factor = 1.0 / math.sqrt(HS)
    keep = live[span] > 0
    for head in range(q_ref.shape[1] // HS):
        cols = slice(head * HS, (head + 1) * HS)
        query = q_ref[:, cols]
        keys = jnp.concatenate([k0_ref[0, :, cols], k1_ref[0, :, cols]], axis=0)
        values = jnp.concatenate([v0_ref[0, :, cols], v1_ref[0, :, cols]], axis=0)
        scores = (
            lax.dot_general(
                query, keys, (((1,), (1,)), ((), ())), preferred_element_type=jnp.float32
            )
            * factor
        )
        weights = jnp.exp(scores - jnp.max(scores, axis=1, keepdims=True))
        total = jnp.sum(weights, axis=1, keepdims=True)
        summed = jnp.dot(
            weights.astype(jnp.bfloat16), values, preferred_element_type=jnp.float32
        )
        merged = summed / total
        out_ref[:, cols] = jnp.where(keep, merged, 0.0).astype(jnp.bfloat16)


def attention(slots, live, grouped, key_rows, value_rows):
    rows, width = grouped.shape
    spans = rows // SPAN

    def block(which):
        return pl.BlockSpec(
            (1, NBR, width), lambda span, slots, live: (slots[2 * span + which], 0, 0)
        )

    token_block = pl.BlockSpec((SPAN, width), lambda span, slots, live: (span, 0))
    return pl.pallas_call(
        attention_kernel,
        grid_spec=pltpu.PrefetchScalarGridSpec(
            num_scalar_prefetch=2,
            grid=(spans,),
            in_specs=[token_block, block(0), block(1), block(0), block(1)],
            out_specs=token_block,
        ),
        out_shape=jax.ShapeDtypeStruct((rows, width), jnp.bfloat16),
        compiler_params=pltpu.CompilerParams(vmem_limit_bytes=24 * 2**20),
        cost_estimate=pl.CostEstimate(
            flops=8 * rows * NBR * width,
            bytes_accessed=4 * rows * width + 8 * spans * NBR * width,
            transcendentals=2 * rows * NBR * width // HS,
        ),
    )(slots, live, grouped, key_rows, key_rows, value_rows, value_rows)


def weights_kernel(slots, q_ref, k0_ref, k1_ref, out_ref):
    factor = 1.0 / math.sqrt(HS)
    for head in range(q_ref.shape[1] // HS):
        cols = slice(head * HS, (head + 1) * HS)
        keys = jnp.concatenate([k0_ref[0, :, cols], k1_ref[0, :, cols]], axis=0)
        scores = (
            lax.dot_general(
                q_ref[:, cols],
                keys,
                (((1,), (1,)), ((), ())),
                preferred_element_type=jnp.float32,
            )
            * factor
        )
        weights = jnp.exp(scores - jnp.max(scores, axis=1, keepdims=True))
        total = jnp.sum(weights, axis=1, keepdims=True)
        place = slice(head * 2 * NBR, (head + 1) * 2 * NBR)
        out_ref[:, place] = (weights * (1.0 / total)).astype(jnp.bfloat16)


def values_kernel(slots, live, weights_ref, v0_ref, v1_ref, out_ref):
    keep = live[pl.program_id(0)] > 0
    for head in range(out_ref.shape[1] // HS):
        cols = slice(head * HS, (head + 1) * HS)
        values = jnp.concatenate([v0_ref[0, :, cols], v1_ref[0, :, cols]], axis=0)
        place = slice(head * 2 * NBR, (head + 1) * 2 * NBR)
        merged = jnp.dot(weights_ref[:, place], values, preferred_element_type=jnp.float32)
        out_ref[:, cols] = jnp.where(keep, merged, 0.0).astype(jnp.bfloat16)


def weigh(slots, queries, key_rows):
    rows, width = queries.shape
    spans = rows // SPAN
    spread = width // HS * 2 * NBR

    def block(which):
        return pl.BlockSpec((1, NBR, width), lambda span, slots: (slots[2 * span + which], 0, 0))

    return pl.pallas_call(
        weights_kernel,
        grid_spec=pltpu.PrefetchScalarGridSpec(
            num_scalar_prefetch=1,
            grid=(spans,),
            in_specs=[
                pl.BlockSpec((SPAN, width), lambda span, slots: (span, 0)),
                block(0),
                block(1),
            ],
            out_specs=pl.BlockSpec((SPAN, spread), lambda span, slots: (span, 0)),
        ),
        out_shape=jax.ShapeDtypeStruct((rows, spread), jnp.bfloat16),
        compiler_params=pltpu.CompilerParams(vmem_limit_bytes=24 * 2**20),
        cost_estimate=pl.CostEstimate(
            flops=4 * rows * NBR * width,
            bytes_accessed=2 * rows * width + 4 * spans * NBR * width + 2 * rows * spread,
            transcendentals=rows * spread,
        ),
    )(slots, queries, key_rows, key_rows)


def combine(slots, live, weights, value_rows):
    rows, spread = weights.shape
    spans = rows // SPAN
    width = value_rows.shape[2]

    def block(which):
        return pl.BlockSpec(
            (1, NBR, width), lambda span, slots, live: (slots[2 * span + which], 0, 0)
        )

    return pl.pallas_call(
        values_kernel,
        grid_spec=pltpu.PrefetchScalarGridSpec(
            num_scalar_prefetch=2,
            grid=(spans,),
            in_specs=[
                pl.BlockSpec((SPAN, spread), lambda span, slots, live: (span, 0)),
                block(0),
                block(1),
            ],
            out_specs=pl.BlockSpec((SPAN, width), lambda span, slots, live: (span, 0)),
        ),
        out_shape=jax.ShapeDtypeStruct((rows, width), jnp.bfloat16),
        compiler_params=pltpu.CompilerParams(vmem_limit_bytes=24 * 2**20),
        cost_estimate=pl.CostEstimate(
            flops=4 * rows * NBR * width,
            bytes_accessed=2 * rows * width + 4 * spans * NBR * width + 2 * rows * spread,
            transcendentals=0,
        ),
    )(slots, live, weights, value_rows, value_rows)


def project_kernel(
    term_ref, w_ref, hidden_ref, out_ref, held, w_held, send_sem, recv_sem, w_sem
):
    me = lax.axis_index("mp")
    count = lax.axis_size("mp")
    width = hidden_ref.shape[1]
    chunks = held.shape[2]
    rows = held.shape[3]

    def fetch(dest):
        cols = pl.ds(pl.multiple_of(dest * width, width), width)
        return pltpu.make_async_copy(w_ref.at[:, cols], w_held.at[dest], w_sem.at[dest])

    for turn in range(count):
        fetch(count - 1 - turn // 2 if turn % 2 == 0 else turn // 2).start()

    barrier = pltpu.get_barrier_semaphore()

    @pl.when(me > 0)
    def _():
        pl.semaphore_signal(
            barrier, inc=1, device_id={"mp": me - 1}, device_id_type=pl.DeviceIdType.MESH
        )

    @pl.when(me < count - 1)
    def _():
        pl.semaphore_signal(
            barrier, inc=1, device_id={"mp": me + 1}, device_id_type=pl.DeviceIdType.MESH
        )

    has_both = jnp.logical_and(me > 0, me < count - 1)

    @pl.when(has_both)
    def _():
        pl.semaphore_wait(barrier, 2)

    @pl.when(jnp.logical_not(has_both))
    def _():
        pl.semaphore_wait(barrier, 1)

    def copy(way, turn, chunk, peer):
        return pltpu.make_async_remote_copy(
            src_ref=held.at[way, turn, chunk],
            dst_ref=held.at[way, turn, chunk],
            send_sem=send_sem.at[way, turn, chunk],
            recv_sem=recv_sem.at[way, turn, chunk],
            device_id={"mp": peer},
            device_id_type=pl.DeviceIdType.MESH,
        )

    def own(chunk, dest):
        first = pl.multiple_of(chunk * rows, rows)
        return jnp.dot(
            term_ref[pl.ds(first, rows), :], w_held[dest], preferred_element_type=jnp.float32
        )

    def pass_on(way, turn, chunk, dest, behind, ahead, has_behind):
        @pl.when(chunk == 0)
        def _():
            fetch(dest).wait()

        part = own(chunk, dest)

        @pl.when(has_behind)
        def _():
            copy(way, turn, chunk, behind).wait_recv()
            held[way, turn, chunk] = (
                part + held[way, turn, chunk].astype(jnp.float32)
            ).astype(jnp.bfloat16)

        @pl.when(jnp.logical_not(has_behind))
        def _():
            held[way, turn, chunk] = part.astype(jnp.bfloat16)

        before = turn * chunks + chunk - DEPTH

        @pl.when(before >= 0)
        def _():
            copy(way, before // chunks, before % chunks, ahead).wait_send()

        copy(way, turn, chunk, ahead).start()

    def step(tick, carry):
        up_index = tick - me
        down_index = tick - (count - 1 - me)

        @pl.when(jnp.logical_and(up_index >= 0, up_index < (count - 1 - me) * chunks))
        def _():
            turn = up_index // chunks
            pass_on(
                0, turn, up_index % chunks, count - 1 - turn, me - 1, me + 1, me > 0
            )

        @pl.when(jnp.logical_and(down_index >= 0, down_index < me * chunks))
        def _():
            turn = down_index // chunks
            pass_on(1, turn, down_index % chunks, turn, me + 1, me - 1, me < count - 1)

        return carry

    lax.fori_loop(0, (count - 1) * chunks, step, 0)
    fetch(me).wait()

    def finish_own(chunk, carry):
        here = pl.ds(pl.multiple_of(chunk * rows, rows), rows)
        out_ref[here, :] = own(chunk, me) + hidden_ref[here, :].astype(jnp.float32)
        return carry

    lax.fori_loop(0, chunks, finish_own, 0)

    def finish(chunk, carry):
        here = pl.ds(pl.multiple_of(chunk * rows, rows), rows)

        @pl.when(me > 0)
        def _():
            copy(0, count - 1 - me, chunk, me - 1).wait_recv()
            out_ref[here, :] += held[0, count - 1 - me, chunk].astype(jnp.float32)

        @pl.when(me < count - 1)
        def _():
            copy(1, me, chunk, me + 1).wait_recv()
            out_ref[here, :] += held[1, me, chunk].astype(jnp.float32)

        return carry

    lax.fori_loop(0, chunks, finish, 0)

    def sent(index, carry):
        turn = index // chunks
        chunk = index % chunks
        ups = (count - 1 - me) * chunks
        downs = me * chunks

        @pl.when(jnp.logical_and(index < ups, index >= ups - DEPTH))
        def _():
            copy(0, turn, chunk, me + 1).wait_send()

        @pl.when(jnp.logical_and(index < downs, index >= downs - DEPTH))
        def _():
            copy(1, turn, chunk, me - 1).wait_send()

        return carry

    lax.fori_loop(0, (count - 1) * chunks, sent, 0)


def project(terms, w_out, hidden):
    tokens, width = hidden.shape
    inner = terms.shape[1]
    count = lax.axis_size("mp")
    chunks = 4
    rows = tokens // chunks
    vmem = pl.BlockSpec(memory_space=pltpu.VMEM)
    return pl.pallas_call(
        project_kernel,
        out_shape=jax.ShapeDtypeStruct((tokens, width), jnp.float32),
        in_specs=[vmem, pl.BlockSpec(memory_space=pl.ANY), vmem],
        out_specs=vmem,
        scratch_shapes=[
            pltpu.VMEM((2, count - 1, chunks, rows, width), jnp.bfloat16),
            pltpu.VMEM((count, inner, width), jnp.bfloat16),
            pltpu.SemaphoreType.DMA((2, count - 1, chunks)),
            pltpu.SemaphoreType.DMA((2, count - 1, chunks)),
            pltpu.SemaphoreType.DMA((count,)),
        ],
        compiler_params=pltpu.CompilerParams(
            collective_id=0, has_side_effects=True, vmem_limit_bytes=56 * 2**20
        ),
        cost_estimate=pl.CostEstimate(
            flops=2 * tokens * inner * width * count,
            bytes_accessed=2 * inner * width * count + 8 * tokens * width,
            transcendentals=0,
        ),
    )(terms, w_out, hidden)


def shards(hidden, norm_gain, w_query, w_out, nb_keys, nb_values, neighbours, valid_spans):
    tok_rows = hidden.shape[0]
    span_dev = tok_rows // SPAN
    stored = nb_keys.shape[0]
    inner_width = w_query.shape[1]
    peer_count = lax.axis_size("dp")
    most_slots = max(2, (2 * span_dev + peer_count - 1) // peer_count)
    widened = lax.all_gather(hidden, "mp", axis=1, tiled=True).astype(jnp.float32)
    normed = (
        widened * lax.rsqrt(jnp.mean(widened * widened, axis=1, keepdims=True) + eps) * norm_gain
    ).astype(jnp.bfloat16)
    queries = jnp.dot(normed, w_query, preferred_element_type=jnp.float32).astype(jnp.bfloat16)
    live_span = jnp.arange(span_dev, dtype=jnp.int32) < valid_spans[0]
    owners = (neighbours // stored).reshape(-1)
    slot_ids = (neighbours % stored).reshape(-1)
    is_live = jnp.repeat(live_span, 2)
    req_order = jnp.arange(owners.shape[0], dtype=jnp.int32)
    earlier = (
        (owners[:, None] == owners[None, :])
        & is_live[None, :]
        & (req_order[None, :] < req_order[:, None])
    )
    slot_rank = jnp.minimum(jnp.sum(earlier.astype(jnp.int32), axis=1), most_slots - 1)
    target = jnp.where(is_live, owners * most_slots + slot_rank, -1)
    slot_match = target[:, None] == jnp.arange(peer_count * most_slots, dtype=jnp.int32)[None, :]
    filled = jnp.any(slot_match, axis=0)
    request_table = jnp.where(
        filled, jnp.sum(jnp.where(slot_match, slot_ids[:, None], 0), axis=0), -1
    )
    request_table = request_table.reshape(peer_count, most_slots)
    safe_ids = jnp.maximum(
        lax.all_to_all(request_table, "dp", split_axis=0, concat_axis=0, tiled=True), 0
    )
    keys_back = lax.all_to_all(nb_keys[safe_ids], "dp", split_axis=0, concat_axis=0, tiled=True)
    wanted, keys_back = lax.optimization_barrier((nb_values[safe_ids], keys_back))
    values_back = lax.all_to_all(wanted, "dp", split_axis=0, concat_axis=0, tiled=True)
    flat_slots = (peer_count * most_slots, NBR, inner_width)
    key_rows = keys_back.reshape(flat_slots)
    value_rows = values_back.reshape(flat_slots)
    slots = owners * most_slots + slot_rank
    live = live_span.astype(jnp.int32)
    split = 2 * (span_dev - 1)
    weights = weigh(slots[:split], queries[SPAN - 1 : tok_rows - 1], key_rows)
    edge, weights = lax.optimization_barrier((queries[: SPAN - 1], weights))
    following = shifted(edge, "dp", -1)
    crossing = jnp.concatenate([queries[tok_rows - 1 :], following], axis=0)
    last = attention(slots[split:], live[span_dev - 1 :], crossing, key_rows, value_rows)
    previous = shifted(last[1:], "dp", 1)
    merged = combine(slots[:split], live[: span_dev - 1], weights, value_rows)
    placed = jnp.concatenate([previous, merged, last[:1]], axis=0)
    return project(placed, w_out, hidden)


def solution(mesh):
    placed = (
        P("dp", "mp"),
        P(),
        P(None, "mp"),
        P("mp", None),
        P("dp", None, "mp"),
        P("dp", None, "mp"),
        P("dp", None),
        P("dp"),
    )
    return jax.shard_map(
        shards, mesh=mesh, in_specs=placed, out_specs=P("dp", "mp"), check_vma=False
    )
```
